256 devices in a mesh: blk: 128 (over x, y, z), ch: 2 (over core).
Axes of the slice: x: 4, y: 4, z: 8, core: 2. Of those that a mesh axis runs over, the one named last changes fastest.
Arguments:
- raw: float32 [2048, 8, 2, 4096], P('blk', 'ch'), may hold values from -6 to 6
- range_filter: float32 [2, 4096], replicated, may hold values from -6 to 6
- recon: float32 [2, 8, 2048], replicated, may hold values from -5 to 5
- rcmc_coef: float32 [8, 2048], replicated, may hold values from -6 to 6
- band_offset: int32 [4096], P(('blk', 'ch')), may hold values from -8 to 7, as said below
- band_width: int32 [4096], P(('blk', 'ch')), may hold values from 1 to 8
- az_filter: float32 [2, 2048, 4096], P(None, None, ('blk', 'ch')), may hold values from -6 to 6
Outputs:
- image: float32 [2, 2048, 4096], P(None, None, ('blk', 'ch'))
The draws below stay inside these ranges and needn't reach their ends.
Inputs may be any that keep to these rules, and one draw needn't show every extreme that they name: band_offset + band_width <= 8 for every bin.
All inputs are finite; a program needn't handle non-finite values.
Results may differ from the reference program's by a relative error of at most 0.0001.
Values sent between devices are 32-bit elements; how exact they have to be, the bound alone decides.
No kernel may reach another device: no remote copies, remote signals or barrier semaphores. Data moves between devices by JAX's collectives and lax.ppermute only.
A program may use at most 128 MiB of HBM per device.

```python
import jax
import jax.numpy as jnp
from jax import lax

CH = 8
RANGE = 4096
AZ = 2048
REACH = 8


def band_draw(key):
    width_key, offset_key = jax.random.split(key)
    widths = jax.random.randint(width_key, (RANGE,), 1, REACH + 1)
    spread = jax.random.randint(offset_key, (RANGE,), 0, 2 * REACH)
    position = jnp.arange(RANGE, dtype=jnp.int32) % 64
    widths = jnp.where(position == 0, REACH, widths)
    widths = jnp.where((position == 1) | (position == 2), 1, widths)
    offsets = spread % (2 * REACH - widths + 1) - REACH
    offsets = jnp.where(position == 1, -REACH, offsets)
    offsets = jnp.where(position == 2, REACH - 1, offsets)
    return (offsets.astype(jnp.int32), widths.astype(jnp.int32))


def draw_band_offset(key, part):
    return band_draw(key)[0]


def draw_band_width(key, part):
    return band_draw(key)[1]


def shard_levels(key, shape, shards, low, high):
    loudness = 1.0
    for dim, parts in shards:
        draws = jax.random.uniform(jax.random.fold_in(jax.random.fold_in(key, 6), dim), (parts,), jnp.float32, low / len(shards), high / len(shards))
        loudness = loudness * jnp.repeat(jnp.exp(draws), shape[dim] // parts).reshape((-1,) + (1,) * (len(shape) - 1 - dim))
    return loudness


def scatter_about(rng, shape, scale, most, cuts=(), held_as=jnp.bfloat16):
    level = shard_levels(rng, shape, cuts, -0.22, 0.18) if cuts else 1.0
    entries = jax.random.normal(rng, shape, jnp.float32) * scale * level
    return jnp.minimum(jnp.maximum(entries, -most), most).astype(held_as)


def setup_inputs(seed: int = 0) -> dict:
    keys = jax.random.split(jax.random.key(seed), 8)
    return {
        "raw": scatter_about(keys[0], (AZ, CH, 2, RANGE), 1.0, 6.0, ((0, 128), (1, 2)), jnp.float32),
        "range_filter": scatter_about(keys[1], (2, RANGE), 1.0, 6.0, (), jnp.float32),
        "recon": scatter_about(keys[2], (2, CH, AZ), 0.35, 5.0, (), jnp.float32),
        "rcmc_coef": scatter_about(keys[3], (REACH, AZ), 0.5, 6.0, (), jnp.float32),
        "band_offset": draw_band_offset(jax.random.fold_in(keys[7], 71), 0),
        "band_width": draw_band_width(jax.random.fold_in(keys[7], 71), 0),
        "az_filter": scatter_about(keys[6], (2, AZ, RANGE), 1.0, 6.0, ((2, 256),), jnp.float32),
    }


def reference(raw, range_filter, recon, rcmc_coef, band_offset, band_width, az_filter):
    reply = lax.complex(range_filter[0], range_filter[1])
    mixed = None
    for channel in range(CH):
        signal = lax.complex(raw[:, channel, 0, :], raw[:, channel, 1, :])
        squeezed = jnp.fft.ifft(jnp.fft.fft(signal, axis=1) * reply[None, :], axis=1)
        doppler = jnp.fft.fft(squeezed, axis=0)
        weights = lax.complex(recon[0, channel], recon[1, channel])
        contribution = weights[:, None] * doppler
        mixed = contribution if mixed is None else mixed + contribution
    padded = jnp.pad(mixed, ((0, 0), (REACH, REACH)))
    bins = jnp.arange(RANGE, dtype=jnp.int32)
    migrated = jnp.zeros_like(mixed)
    for tap_step in range(REACH):
        source = jnp.minimum(bins + REACH + band_offset + tap_step, RANGE + 2 * REACH - 1).astype(jnp.int32)
        taken = jnp.take(padded, source, axis=1)
        living = (tap_step < band_width)[None, :]
        migrated = migrated + jnp.where(living, rcmc_coef[tap_step][:, None] * taken, 0.0)
    focused = jnp.fft.ifft(migrated * lax.complex(az_filter[0], az_filter[1]), axis=0)
    return jnp.stack([jnp.real(focused), jnp.imag(focused)]).astype(jnp.float32)
```

```python
import functools
import math

import jax
import jax.numpy as jnp
import ml_dtypes
import numpy as np
from jax import lax
from jax.experimental import pallas as pl
from jax.experimental.pallas import tpu as pltpu
from jax.sharding import PartitionSpec as P

REACH = 8
BF16 = jnp.bfloat16
F32 = jnp.float32
PARTS = (4,)
RANGE_VMEM = 60 * 2**20
CHIP = np.arange(128).reshape(4, 4, 8).transpose(0, 2, 1).reshape(128)
PLACE = np.argsort(CHIP)
TURN = ("x", "z", "y")
BLK = ("x", "y", "z")
EVERY = ("x", "y", "z", "ch")


def phase(rows, cols, length, sign):
    angle = sign * 2.0 * np.pi * ((np.outer(rows, cols) % length) / length)
    return np.cos(angle), np.sin(angle)


def pair(table):
    high = table.astype(np.float32).astype(ml_dtypes.bfloat16)
    low = (table - high.astype(np.float64)).astype(np.float32).astype(ml_dtypes.bfloat16)
    return high, low


def as_left(table):
    high, low = pair(table)
    return np.concatenate([high, high, low], axis=1)


def as_right(table):
    high, low = pair(table)
    return np.concatenate([high, high, low], axis=0)


def right_matrix(cosine, sine, scale=1.0):
    return np.block([[cosine, sine], [-sine, cosine]]) * scale


@functools.cache
def range_tables():
    t = np.arange(32)
    lane = np.arange(128)
    c32, s32 = phase(t, t, 32, -1)
    left = np.zeros((64, 32, 2))
    left[:32, :, 0], left[:32, :, 1] = c32, -s32
    left[32:, :, 0], left[32:, :, 1] = s32, c32
    first = as_left(left.reshape(64, 64))
    twist_in = np.stack(phase(t, lane, 4096, -1)).astype(np.float32)
    kl = 4 * (lane % 32) + lane // 32
    second = as_right(right_matrix(*phase(lane, kl, 128, -1)))
    third = as_right(right_matrix(*phase(kl, lane, 128, 1), scale=1.0 / 4096))
    twist_out = np.stack(phase(t, lane, 4096, 1)).astype(np.float32)
    c32, s32 = phase(t, t, 32, 1)
    wide = np.zeros((32, 2, 4, 4, 2, 32))
    for line in range(4):
        wide[:, 0, line, line, 0], wide[:, 0, line, line, 1] = c32, -s32
        wide[:, 1, line, line, 0], wide[:, 1, line, line, 1] = s32, c32
    last = as_left(wide.reshape(256, 256))
    first = np.pad(first, ((0, 0), (0, 64)))
    last = last.reshape(256, 3, 256).transpose(1, 0, 2).reshape(768, 256)
    matrices = np.concatenate([second, third, last, first], axis=0)
    return matrices, np.concatenate([twist_in, twist_out], axis=0)


@functools.cache
def line_tables():
    row = np.arange(128)
    fb = 16 * (row % 8) + row // 8
    out = []
    for j in range(16):
        source = 16 * CHIP + j
        c, s = phase(fb, source, 2048, -1)
        high, low = pair(np.block([[c, -s], [s, c]]))
        out.append(np.concatenate([high, low], axis=1))
    eye = np.eye(128).astype(ml_dtypes.bfloat16)
    return np.stack(out), np.concatenate([eye, eye], axis=1)


@functools.cache
def focus_tables():
    lane = np.arange(128)
    right = as_right(right_matrix(*phase(lane, lane, 128, 1), scale=1.0 / 2048))
    twist = np.stack(phase(np.arange(16), lane, 2048, 1)).astype(np.float32)
    return right, twist


def split(x):
    high = x.astype(BF16)
    return high, (x - high.astype(F32)).astype(BF16)


def dot(left, right):
    return jnp.dot(left, right, preferred_element_type=F32)


def left_rows(re, im):
    rh, rl = split(re)
    ih, il = split(im)
    return jnp.concatenate([rh, ih, rl, il, rh, ih], axis=1)


def right_cols(x):
    high, low = split(x)
    return jnp.concatenate([high, low, high], axis=0)


def times(ar, ai, br, bi):
    return ar * br - ai * bi, ar * bi + ai * br


def small_fft(values, sign):
    count = len(values)
    if count == 1:
        return values
    even = small_fft(values[0::2], sign)
    odd = small_fft(values[1::2], sign)
    low, high = [], []
    for k in range(count // 2):
        (er, ei), (pr, pi) = even[k], odd[k]
        if k == 0:
            tr, ti = pr, pi
        elif 4 * k == count:
            tr, ti = (-pi, pr) if sign > 0 else (pi, -pr)
        else:
            c, s = math.cos(2 * math.pi * k / count), sign * math.sin(2 * math.pi * k / count)
            tr, ti = pr * c - pi * s, pr * s + pi * c
        low.append((er + tr, ei + ti))
        high.append((er - tr, ei - ti))
    return low + high


def swap_blocks(parts):
    lane = lax.broadcasted_iota(jnp.int32, parts[0].shape, 1)
    low = lane < 64
    a, b, c, d = parts

    def halves(p, q):
        return (
            jnp.where(low, p, pltpu.roll(q, 64, 1)),
            jnp.where(low, pltpu.roll(p, 64, 1), q),
        )

    a, c = halves(a, c)
    b, d = halves(b, d)
    even = (lane // 32) % 2 == 0

    def quarters(p, q):
        return (
            jnp.where(even, p, pltpu.roll(q, 32, 1)),
            jnp.where(even, pltpu.roll(p, 96, 1), q),
        )

    a, b = quarters(a, b)
    c, d = quarters(c, d)
    return a, b, c, d


def range_kernel(raw, filt, matrices, twists, out, held):
    @pl.when(pl.program_id(0) == 0)
    def _():
        for part in range(2):
            rows = filt[pl.ds(part, 32, stride=2), :]
            tall = jnp.concatenate([rows, jnp.zeros((96, 128), F32)], axis=0).T
            total = tall[0:32]
            for m in range(1, 4):
                total = total + pltpu.roll(tall[32 * m : 32 * m + 32], 32 * m, 1)
            held[part] = total

    count = raw.shape[0]
    second, third = matrices[0:768, :], matrices[768:1536, :]
    last = jnp.concatenate([matrices[1536 + 256 * i : 1792 + 256 * i, :] for i in range(3)], axis=1)
    first = matrices[2304:2368, :][:, :192]
    tr = jnp.concatenate([twists[0]] * 2, axis=1)
    ti = jnp.concatenate([twists[1]] * 2, axis=1)
    res, ims = [], []
    for i in range(0, count, 2):
        x = jnp.concatenate([raw[i], raw[i + 1]], axis=1)
        y = dot(first, right_cols(x))
        zr, zi = times(y[:32], y[32:], tr, ti)
        res += [zr[:, :128], zr[:, 128:]]
        ims += [zi[:, :128], zi[:, 128:]]
    spectrum = dot(
        left_rows(jnp.concatenate(res, axis=0), jnp.concatenate(ims, axis=0)), second
    )
    sr = spectrum[:, :128].reshape(count, 32, 128)
    si = spectrum[:, 128:].reshape(count, 32, 128)
    sr, si = times(sr, si, held[0][None], held[1][None])
    back = dot(left_rows(sr.reshape(count * 32, 128), si.reshape(count * 32, 128)), third)
    br = back[:, :128].reshape(count, 32, 128)
    bi = back[:, 128:].reshape(count, 32, 128)
    br, bi = times(br, bi, twists[2][None], twists[3][None])
    done = []
    for c in range(0, 4, 2):
        cols = []
        for cc in (c, c + 1):
            rows = []
            for line in range(4):
                rows += [br[line * 4 + cc], bi[line * 4 + cc]]
            cols.append(jnp.concatenate(rows, axis=0))
        y = dot(last, right_cols(jnp.concatenate(cols, axis=1)))
        done += [y[:, :128], y[:, 128:]]
    for q, block in enumerate(swap_blocks(done)):
        for nt in range(32):
            out[int(PLACE[4 * nt + q])] = block[8 * nt : 8 * nt + 8]


def compress(raw_rows, filt_rows, start, groups):
    matrices, twists = range_tables()
    return pl.pallas_call(
        range_kernel,
        grid=(groups,),
        in_specs=[
            pl.BlockSpec((16, 64, 128), lambda g: (g + start, 0, 0)),
            pl.BlockSpec((64, 128), lambda g: (0, 0)),
            pl.BlockSpec(matrices.shape, lambda g: (0, 0)),
            pl.BlockSpec(twists.shape, lambda g: (0, 0, 0)),
        ],
        out_specs=pl.BlockSpec((128, 8, 128), lambda g: (0, g, 0)),
        out_shape=jax.ShapeDtypeStruct((128, 8 * groups, 128), F32),
        scratch_shapes=[pltpu.VMEM((2, 32, 128), F32)],
        compiler_params=pltpu.CompilerParams(vmem_limit_bytes=RANGE_VMEM),
        cost_estimate=pl.CostEstimate(
            flops=10**9 * groups, bytes_accessed=2**20 * groups, transcendentals=0
        ),
        name="range_compress",
    )(raw_rows, filt_rows, matrices, twists)


def transform_lines(turned, table, put):
    for jj in range(4):
        x = jnp.concatenate([turned[:, jj, :], turned[:, 4 + jj, :]], axis=0)
        f = table[jj]
        put(jj, dot(jnp.concatenate([f[:, :256], f], axis=1), right_cols(x)))


def line_kernel(turned, table, out):
    def put(jj, y):
        out[jj] = y

    transform_lines(turned, table, put)


def doppler_part(turned, start):
    table, _ = line_tables()
    groups = turned.shape[1] // 8
    return pl.pallas_call(
        line_kernel,
        grid=(groups,),
        in_specs=[
            pl.BlockSpec((128, 8, 128), lambda g: (0, g, 0)),
            pl.BlockSpec((4, 256, 512), lambda g: (g + start, 0, 0)),
        ],
        out_specs=pl.BlockSpec((4, 256, 128), lambda g: (g, 0, 0)),
        out_shape=jax.ShapeDtypeStruct((4 * groups, 256, 128), F32),
        compiler_params=pltpu.CompilerParams(vmem_limit_bytes=32 * 2**20),
        cost_estimate=pl.CostEstimate(
            flops=10**9 * groups, bytes_accessed=2**20 * groups, transcendentals=0
        ),
        name="doppler_part",
    )(turned, table)


def mix_kernel(count, ch, turned, table, eye, weights, *refs):
    earlier, (own, send, near, far, held) = refs[:count], refs[count:]
    group = pl.program_id(0)

    def put(jj, y):
        held[group * 4 + jj] = y

    transform_lines(turned, table, put)

    @pl.when(group == pl.num_programs(0) - 1)
    def _():
        first = ch[0] == 0

        def step(q, carry):
            rows = pl.ds(pl.multiple_of(q * 8, 8), 8)
            later = pl.ds(pl.multiple_of(128 + q * 8, 8), 8)
            lines = []
            for ref in (*earlier, held):
                lines += [(ref[j, rows, :], ref[j, later, :]) for j in range(ref.shape[0])]
            spectrum = small_fft(lines, -1)
            re = jnp.concatenate([v[0] for v in spectrum], axis=0)
            im = jnp.concatenate([v[1] for v in spectrum], axis=0)
            high, low = split(jnp.concatenate([re, im], axis=0))
            flat = lax.dot_general(
                eye[...],
                jnp.concatenate([high, low], axis=1),
                (((1,), (1,)), ((), ())),
                preferred_element_type=F32,
            )
            mr = mi = None
            for c in range(4):
                dr, di = flat[32 * c : 32 * c + 32, :128], flat[32 * c : 32 * c + 32, 128:]
                wr, wi = weights[0, c, pl.ds(q, 1), :], weights[1, c, pl.ds(q, 1), :]
                pr, pi = times(dr, di, wr, wi)
                mr, mi = (pr, pi) if mr is None else (mr + pr, mi + pi)
            for part, m in enumerate((mr, mi)):
                low24, high24 = m[:24], m[8:]
                own[q, part] = jnp.where(first, low24, high24)
                send[q, part] = jnp.where(first, high24, low24)
                near[q, part] = jnp.where(first, m[:8], m[24:])
                far[q, part] = jnp.where(first, m[24:], m[:8])
            return carry

        lax.fori_loop(0, 16, step, 0)


def doppler_mix(ch, turned, start, earlier, weights):
    table, eye = line_tables()
    groups = turned.shape[1] // 8
    wide = jax.ShapeDtypeStruct((16, 2, 24, 128), F32)
    thin = jax.ShapeDtypeStruct((16, 2, 8, 128), F32)
    whole = lambda n: (lambda g, *_: (0,) * n)
    return pl.pallas_call(
        functools.partial(mix_kernel, len(earlier)),
        grid_spec=pltpu.PrefetchScalarGridSpec(
            num_scalar_prefetch=1,
            grid=(groups,),
            in_specs=[
                pl.BlockSpec((128, 8, 128), lambda g, *_: (0, g, 0)),
                pl.BlockSpec((4, 256, 512), lambda g, *_: (g + start, 0, 0)),
                pl.BlockSpec((128, 256), whole(2)),
                pl.BlockSpec((2, 4, 16, 128), whole(4)),
                *[pl.BlockSpec(e.shape, whole(3)) for e in earlier],
            ],
            out_specs=[
                pl.BlockSpec(wide.shape, whole(4)),
                pl.BlockSpec(wide.shape, whole(4)),
                pl.BlockSpec(thin.shape, whole(4)),
                pl.BlockSpec(thin.shape, whole(4)),
            ],
            scratch_shapes=[pltpu.VMEM((4 * groups, 256, 128), F32)],
        ),
        out_shape=[wide, wide, thin, thin],
        compiler_params=pltpu.CompilerParams(vmem_limit_bytes=32 * 2**20),
        cost_estimate=pl.CostEstimate(
            flops=10**9 * groups, bytes_accessed=2**20 * groups, transcendentals=0
        ),
        name="doppler_mix",
    )(ch, turned, table, eye, weights, *earlier)


def focus_kernel(own, got, near, far, select, coef, az, right, twist, out, held):
    def step(q, carry):
        cols = []
        for part in range(2):
            cols.append(
                jnp.concatenate([own[q, part] + got[q, part], near[q, part] + far[q, part]], axis=0)
            )
        high, low = split(jnp.concatenate(cols, axis=1))
        taps = dot(select[...], jnp.concatenate([high, low], axis=0))
        moved = None
        for k in range(REACH):
            scale = coef[k, pl.ds(q, 1), :]
            term = taps[16 * k : 16 * k + 16] * jnp.concatenate([scale, scale], axis=1)
            moved = term if moved is None else moved + term
        fr, fi = times(moved[:, :128], moved[:, 128:], az[0, q], az[1, q])
        rows = pl.ds(pl.multiple_of(q * 16, 16), 16)
        held[0, rows, :] = fr
        held[1, rows, :] = fi
        return carry

    lax.fori_loop(0, 16, step, 0)
    y = dot(left_rows(held[0], held[1]), right[...])
    values = []
    for q in range(16):
        rows = y[16 * q : 16 * q + 16]
        values.append(times(rows[:, :128], rows[:, 128:], twist[0, q : q + 1], twist[1, q : q + 1]))
    for n, (re, im) in enumerate(small_fft(values, 1)):
        out[0, :, 128 * n : 128 * n + 128] = re
        out[1, :, 128 * n : 128 * n + 128] = im


def focus(own, got, near, far, select, coef, az):
    right, twist = focus_tables()
    return pl.pallas_call(
        focus_kernel,
        out_shape=jax.ShapeDtypeStruct((2, 16, 2048), F32),
        scratch_shapes=[pltpu.VMEM((2, 256, 128), F32)],
        compiler_params=pltpu.CompilerParams(vmem_limit_bytes=48 * 2**20),
        name="focus",
    )(own, got, near, far, select, coef, az, right, twist)


def tap_select(band_offset, band_width, ch):
    tap = jnp.arange(REACH, dtype=jnp.int32)[:, None, None]
    row = (jnp.arange(32, dtype=jnp.int32) + REACH * (1 - ch)) % 32
    target = jnp.arange(16, dtype=jnp.int32)[None, :, None] + REACH + band_offset[None, :, None] + tap
    hit = (row[None, None, :] == target) & (tap < band_width[None, :, None])
    hit = hit.astype(BF16).reshape(REACH * 16, 32)
    return jnp.concatenate([hit, hit], axis=1)


def body(raw, range_filter, recon, rcmc_coef, band_offset, band_width, az_filter):
    ch = lax.axis_index("ch")
    blocks = lax.axis_size(BLK)
    raw_rows = raw.reshape(16, 4, 2, 32, 128).transpose(0, 1, 3, 2, 4).reshape(64, 64, 128)
    filt_rows = range_filter.reshape(2, 32, 128).transpose(1, 0, 2).reshape(64, 128)
    starts = [sum(PARTS[:i]) for i in range(len(PARTS))]
    turned = []
    for i, (start, groups) in enumerate(zip(starts, PARTS)):
        pieces = compress(raw_rows, filt_rows, start, groups)
        if i == 0:
            (pieces, recon, rcmc_coef, az_filter, band_offset) = lax.optimization_barrier(
                (pieces, recon, rcmc_coef, az_filter, band_offset)
            )
        turned.append(lax.all_to_all(pieces, TURN, split_axis=0, concat_axis=0, tiled=True))
    weights = lax.dynamic_slice_in_dim(recon, ch * 4, 4, 1)
    weights = weights.reshape(2, 4, 128, 16).transpose(0, 1, 3, 2)
    coef = rcmc_coef.reshape(REACH, 128, 16).transpose(0, 2, 1)
    az = az_filter.reshape(2, 128, 16, 16).transpose(0, 2, 3, 1)
    select = tap_select(band_offset, band_width, ch)
    earlier = [doppler_part(t, start) for t, start in zip(turned[:-1], starts)]
    last, coef, az, select = lax.optimization_barrier((turned[-1], coef, az, select))
    own, send, near, far = doppler_mix(ch.reshape(1), last, starts[-1], earlier, weights)

    total = 2 * blocks
    cross = [(i, i + 1 if i % 2 else i - 1) for i in range(total)]
    along = [(i, i - 2 if i % 2 else i + 2) for i in range(total)]
    inside = lambda pairs: [(s, d) for s, d in pairs if 0 <= d < total]
    near = lax.ppermute(near, EVERY, inside(cross))
    far = lax.ppermute(far, EVERY, inside(along))
    got = lax.ppermute(send, "ch", [(0, 1), (1, 0)])
    image = focus(own, got, near, far, select, coef, az)
    return image.transpose(0, 2, 1)


def solution(mesh):
    grid = jax.sharding.Mesh(mesh.devices.reshape(4, 4, 8, 2), EVERY)
    return jax.shard_map(
        body,
        mesh=grid,
        in_specs=(
            P(BLK, "ch", None, None),
            P(),
            P(),
            P(),
            P(EVERY),
            P(EVERY),
            P(None, None, EVERY),
        ),
        out_specs=P(None, None, EVERY),
        check_vma=False,
    )
```

```python
import functools
import itertools
import math

import jax
import jax.numpy as jnp
import ml_dtypes
import numpy as np
from jax import lax
from jax.experimental import pallas as pl
from jax.experimental.pallas import tpu as pltpu
from jax.sharding import PartitionSpec as P

REACH = 8
BF16 = jnp.bfloat16
F32 = jnp.float32
RANGE_VMEM = 60 * 2**20
UNROLL = 16
CHIP = np.arange(128).reshape(4, 4, 8).transpose(0, 2, 1).reshape(128)
PLACE = np.argsort(CHIP)
TURN = ("ch", "x", "z", "y")
BLK = ("x", "y", "z")
EVERY = ("x", "y", "z", "ch")


def phase(rows, cols, length, sign):
    angle = sign * 2.0 * np.pi * ((np.outer(rows, cols) % length) / length)
    return np.cos(angle), np.sin(angle)


def pair(table):
    high = table.astype(np.float32).astype(ml_dtypes.bfloat16)
    low = (table - high.astype(np.float64)).astype(np.float32).astype(ml_dtypes.bfloat16)
    return high, low


def as_left(table):
    high, low = pair(table)
    return np.concatenate([high, high, low], axis=1)


def as_right(table):
    high, low = pair(table)
    return np.concatenate([high, high, low], axis=0)


def right_matrix(cosine, sine, scale=1.0):
    return np.block([[cosine, sine], [-sine, cosine]]) * scale


@functools.cache
def range_tables():
    t = np.arange(32)
    lane = np.arange(128)
    c32, s32 = phase(t, t, 32, -1)
    left = np.zeros((64, 32, 2))
    left[:32, :, 0], left[:32, :, 1] = c32, -s32
    left[32:, :, 0], left[32:, :, 1] = s32, c32
    first = as_left(left.reshape(64, 64))
    twist_in = np.stack(phase(t, lane, 4096, -1)).astype(np.float32)
    kl = 4 * (lane % 32) + lane // 32
    second = as_right(right_matrix(*phase(lane, kl, 128, -1)))
    third = as_right(right_matrix(*phase(kl, lane, 128, 1), scale=1.0 / 4096))
    twist_out = np.stack(phase(t, lane, 4096, 1)).astype(np.float32)
    c32, s32 = phase(t, t, 32, 1)
    high, low = pair(np.block([[c32, -s32], [s32, c32]]))
    last = np.block([[high, high], [low, np.zeros_like(low)]])
    last = np.pad(last, ((0, 0), (0, 128)))
    high, low = first[:, :64], first[:, 128:]
    first = np.block([[high, high], [low, np.zeros_like(low)]])
    first = np.pad(first, ((0, 0), (0, 128)))
    matrices = np.concatenate([second, third, last, first], axis=0)
    return matrices, np.concatenate([twist_in, twist_out], axis=0)


@functools.cache
def line_tables():
    row = np.arange(128)
    fb = 16 * (row % 8) + row // 8
    c, s = phase(fb, 16 * CHIP, 2048, -1)
    high, low = pair(np.block([[c, -s], [s, c]]))
    table = np.concatenate([high, low], axis=1)
    twist = np.stack(phase(fb, np.arange(16), 2048, -1)).astype(np.float32)
    eye = np.eye(128).astype(ml_dtypes.bfloat16)
    return table, twist, np.concatenate([eye, eye], axis=1)


@functools.cache
def focus_tables():
    lane = np.arange(128)
    right = as_right(right_matrix(*phase(lane, lane, 128, 1), scale=1.0 / 2048))
    twist = np.stack(phase(np.arange(16), lane, 2048, 1)).astype(np.float32)
    return right, twist


def split(x):
    high = x.astype(BF16)
    return high, (x - high.astype(F32)).astype(BF16)


def dot(left, right):
    return jnp.dot(left, right, preferred_element_type=F32)


def left_rows(re, im):
    rh, rl = split(re)
    ih, il = split(im)
    return jnp.concatenate([rh, ih, rl, il, rh, ih], axis=1)


def right_cols(x):
    high, low = split(x)
    return jnp.concatenate([high, low, high], axis=0)


def times(ar, ai, br, bi):
    return ar * br - ai * bi, ar * bi + ai * br


def small_fft(values, sign):
    count = len(values)
    if count == 1:
        return values
    even = small_fft(values[0::2], sign)
    odd = small_fft(values[1::2], sign)
    low, high = [], []
    for k in range(count // 2):
        (er, ei), (pr, pi) = even[k], odd[k]
        if k == 0:
            tr, ti = pr, pi
        elif 4 * k == count:
            tr, ti = (-pi, pr) if sign > 0 else (pi, -pr)
        else:
            c, s = math.cos(2 * math.pi * k / count), sign * math.sin(2 * math.pi * k / count)
            tr, ti = pr * c - pi * s, pr * s + pi * c
        low.append((er + tr, ei + ti))
        high.append((er - tr, ei - ti))
    return low + high


def swap_blocks(parts):
    lane = lax.broadcasted_iota(jnp.int32, parts[0].shape, 1)
    parts = list(parts)
    for step in (4, 2, 1):
        width = 16 * step
        low = (lane // width) % 2 == 0
        for i in range(8):
            if i & step:
                continue
            p, q = parts[i], parts[i + step]
            m = jnp.where(low, q, p)
            if step == 4:
                m = pltpu.roll(m, 64, 1)
            else:
                m = jnp.take_along_axis(m, lane ^ width, axis=1)
            parts[i] = jnp.where(low, p, m)
            parts[i + step] = jnp.where(low, m, q)
    return parts


def range_kernel(raw, filt, matrices, twists, out, raws, mats, small, reply, kept, held, ready, gone):
    loads = []
    for i, (source, target) in enumerate(
        [
            (matrices.at[1664:1792], mats.at[1664:1792]),
            (raw.at[0:16], raws.at[0:16]),
            (twists, small),
            (filt, reply),
            (matrices.at[0:768], mats.at[0:768]),
            (matrices.at[768:1536], mats.at[768:1536]),
            (matrices.at[1536:1664], mats.at[1536:1664]),
            (raw.at[16:32], raws.at[16:32]),
            (raw.at[32:48], raws.at[32:48]),
            (raw.at[48:64], raws.at[48:64]),
        ]
    ):
        copy = pltpu.make_async_copy(source, target, ready.at[i])
        copy.start()
        loads.append(copy)
    for i in range(4):
        loads[i].wait()
    first = mats[1664:1792, :][:, :128]
    tr = jnp.concatenate([small[0]] * 2, axis=1)
    ti = jnp.concatenate([small[1]] * 2, axis=1)
    turned_filter = []
    for part in range(2):
        rows = reply[pl.ds(part, 32, stride=2), :]
        tall = jnp.concatenate([rows, jnp.zeros((96, 128), F32)], axis=0).T
        total = tall[0:32]
        for m in range(1, 4):
            total = total + pltpu.roll(tall[32 * m : 32 * m + 32], 32 * m, 1)
        turned_filter.append(total)
    hr, hi = turned_filter
    stores = []
    for group in range(4):
        res, ims = [], []
        for i in range(16 * group, 16 * group + 16, 2):
            x = jnp.concatenate([raws[i], raws[i + 1]], axis=1)
            xh, xl = split(x)
            y = dot(first, jnp.concatenate([xh, xl], axis=0))
            y = y[:64] + y[64:]
            zr, zi = times(y[:32], y[32:], tr, ti)
            res += [zr[:, :128], zr[:, 128:]]
            ims += [zi[:, :128], zi[:, 128:]]
        if group == 0:
            for i in range(4, 10):
                loads[i].wait()
        second, third = mats[0:768, :], mats[768:1536, :]
        last = mats[1536:1664, :][:, :128]
        spectrum = dot(
            left_rows(jnp.concatenate(res, axis=0), jnp.concatenate(ims, axis=0)), second
        )
        sr = spectrum[:, :128].reshape(16, 32, 128)
        si = spectrum[:, 128:].reshape(16, 32, 128)
        sr, si = times(sr, si, hr[None], hi[None])
        back = dot(left_rows(sr.reshape(512, 128), si.reshape(512, 128)), third)
        br = back[:, :128].reshape(16, 32, 128)
        bi = back[:, 128:].reshape(16, 32, 128)
        br, bi = times(br, bi, small[2][None], small[3][None])
        for i in range(0, 16, 2):
            cols = [jnp.concatenate([br[k], bi[k]], axis=0) for k in (i, i + 1)]
            xh, xl = split(jnp.concatenate(cols, axis=1))
            y = dot(last, jnp.concatenate([xh, xl], axis=0))
            y = y[:64] + y[64:]
            for k in range(2):
                line, c = (i + k) // 4, (i + k) % 4
                for part in range(2):
                    kept[group % 2, c, pl.ds(part * 4 + line, 32, stride=8), :] = y[
                        32 * part : 32 * part + 32, 128 * k : 128 * k + 128
                    ]
        if group % 2 == 0:
            continue
        half = group // 2
        parts = [kept.at[g, c] for g in range(2) for c in range(4)]
        for i in range(32):
            blocks = swap_blocks([p[8 * i : 8 * i + 8, :] for p in parts])
            for d, block in enumerate(blocks):
                place = int(PLACE[4 * i + d // 2]) + 128 * (d % 2)
                held[half, place] = block
            if i % 8 == 7:
                for core in range(2):
                    spot = 128 * core + 4 * (i - 7)
                    copy = pltpu.make_async_copy(
                        held.at[half, spot : spot + 32],
                        out.at[spot : spot + 32, 8 * half : 8 * half + 8, :],
                        gone.at[len(stores)],
                    )
                    copy.start()
                    stores.append(copy)
    for copy in stores:
        copy.wait()


def compress(raw_rows, filt_rows):
    matrices, twists = range_tables()
    anywhere = pl.BlockSpec(memory_space=pl.ANY)
    return pl.pallas_call(
        range_kernel,
        in_specs=[anywhere] * 4,
        out_specs=anywhere,
        out_shape=jax.ShapeDtypeStruct((256, 16, 128), F32),
        scratch_shapes=[
            pltpu.VMEM((64, 64, 128), F32),
            pltpu.VMEM(matrices.shape, BF16),
            pltpu.VMEM((4, 32, 128), F32),
            pltpu.VMEM((64, 128), F32),
            pltpu.VMEM((2, 4, 256, 128), F32),
            pltpu.VMEM((2, 256, 8, 128), F32),
            pltpu.SemaphoreType.DMA((10,)),
            pltpu.SemaphoreType.DMA((16,)),
        ],
        compiler_params=pltpu.CompilerParams(vmem_limit_bytes=RANGE_VMEM),
        cost_estimate=pl.CostEstimate(flops=4 * 10**9, bytes_accessed=2**22, transcendentals=0),
        name="range_compress",
    )(raw_rows, filt_rows, matrices, twists)


def mix_kernel(ch, turned, table, twist, eye, weights, own, near, far, held):
    low = lax.broadcasted_iota(jnp.int32, (128, 128), 1) < 64
    f = table[...]
    f = jnp.concatenate([f[:, :256], f], axis=1)
    for half, line in itertools.product(range(2), range(4)):
        cols = [
            jnp.concatenate(
                [turned[128 * s : 128 * s + 128, half * 8 + part * 4 + line, :] for s in range(2)], 1
            )
            for part in range(2)
        ]
        y = dot(f, right_cols(jnp.concatenate(cols, axis=0)))
        pairs = []
        for part in range(2):
            a, b = y[128 * part : 128 * part + 128, :128], y[128 * part : 128 * part + 128, 128:]
            m = pltpu.roll(jnp.where(low, b, a), 64, 1)
            pairs.append((jnp.where(low, a, m), jnp.where(low, m, b)))
        for k in range(2):
            j = half * 8 + 4 * k + line
            re, im = pairs[0][k], pairs[1][k]
            if j:
                re, im = times(re, im, twist[0, :, j : j + 1], twist[1, :, j : j + 1])
            held[j, 0] = re
            held[j, 1] = im

    low_core = ch[0] == 0

    def step(q, carry):
        rows = pl.ds(pl.multiple_of(q * 8, 8), 8)
        lines = [(held[j, 0, rows, :], held[j, 1, rows, :]) for j in range(16)]
        spectrum = small_fft(lines, -1)
        re = jnp.concatenate([v[0] for v in spectrum], axis=0)
        im = jnp.concatenate([v[1] for v in spectrum], axis=0)
        high, rest = split(jnp.concatenate([re, im], axis=0))
        flat = lax.dot_general(
            eye[...],
            jnp.concatenate([high, rest], axis=1),
            (((1,), (1,)), ((), ())),
            preferred_element_type=F32,
        )
        mr = mi = None
        for c in range(8):
            dr, di = flat[16 * c : 16 * c + 16, :128], flat[16 * c : 16 * c + 16, 128:]
            wr, wi = weights[0, c, pl.ds(q, 1), :], weights[1, c, pl.ds(q, 1), :]
            pr, pi = times(dr, di, wr, wi)
            mr, mi = (pr, pi) if mr is None else (mr + pr, mi + pi)
        for part, m in enumerate((mr, mi)):
            own[q, part] = m
            near[q, part] = jnp.where(low_core, m[8:], m[:8])
            far[q, part] = jnp.where(low_core, m[:8], m[8:])
        return carry

    lax.fori_loop(0, 16, step, 0, unroll=UNROLL)


def doppler_mix(ch, turned, weights):
    table, twist, eye = line_tables()
    wide = jax.ShapeDtypeStruct((16, 2, 16, 128), F32)
    thin = jax.ShapeDtypeStruct((16, 2, 8, 128), F32)
    inside = pl.BlockSpec(memory_space=pltpu.VMEM)
    return pl.pallas_call(
        mix_kernel,
        in_specs=[pl.BlockSpec(memory_space=pltpu.SMEM)] + [inside] * 5,
        out_specs=[inside] * 3,
        out_shape=[wide, thin, thin],
        scratch_shapes=[pltpu.VMEM((16, 2, 128, 128), F32)],
        compiler_params=pltpu.CompilerParams(vmem_limit_bytes=24 * 2**20),
        cost_estimate=pl.CostEstimate(flops=4 * 10**9, bytes_accessed=2**22, transcendentals=0),
        name="doppler_mix",
    )(ch, turned, table, twist, eye, weights)


def focus_kernel(own, near, far, select, coef, az, right, twist, out, held):
    def step(q, carry):
        cols = []
        for part in range(2):
            cols.append(jnp.concatenate([own[q, part], near[q, part], far[q, part]], axis=0))
        high, low = split(jnp.concatenate(cols, axis=1))
        taps = dot(select[...], jnp.concatenate([high, low], axis=0))
        moved = None
        for k in range(REACH):
            scale = coef[k, pl.ds(q, 1), :]
            term = taps[16 * k : 16 * k + 16] * jnp.concatenate([scale, scale], axis=1)
            moved = term if moved is None else moved + term
        fr, fi = times(moved[:, :128], moved[:, 128:], az[0, q], az[1, q])
        rows = pl.ds(pl.multiple_of(q * 16, 16), 16)
        held[0, rows, :] = fr
        held[1, rows, :] = fi
        return carry

    lax.fori_loop(0, 16, step, 0, unroll=UNROLL)
    y = dot(left_rows(held[0], held[1]), right[...])
    values = []
    for q in range(16):
        rows = y[16 * q : 16 * q + 16]
        values.append(times(rows[:, :128], rows[:, 128:], twist[0, q : q + 1], twist[1, q : q + 1]))
    for n, (re, im) in enumerate(small_fft(values, 1)):
        out[0, :, 128 * n : 128 * n + 128] = re
        out[1, :, 128 * n : 128 * n + 128] = im


def focus(own, near, far, select, coef, az):
    right, twist = focus_tables()
    return pl.pallas_call(
        focus_kernel,
        out_shape=jax.ShapeDtypeStruct((2, 16, 2048), F32),
        scratch_shapes=[pltpu.VMEM((2, 256, 128), F32)],
        compiler_params=pltpu.CompilerParams(vmem_limit_bytes=48 * 2**20),
        name="focus",
    )(own, near, far, select, coef, az, right, twist)


def tap_select(band_offset, band_width, ch):
    tap = jnp.arange(REACH, dtype=jnp.int32)[:, None, None]
    eight = jnp.arange(8, dtype=jnp.int32)
    left, right = eight, eight + 24
    row = jnp.concatenate(
        [
            eight + 8,
            eight + 16,
            jnp.where(ch == 0, right, left),
            jnp.where(ch == 0, left, right),
        ]
    )
    target = jnp.arange(16, dtype=jnp.int32)[None, :, None] + REACH + band_offset[None, :, None] + tap
    hit = (row[None, None, :] == target) & (tap < band_width[None, :, None])
    hit = hit.astype(BF16).reshape(REACH * 16, 32)
    return jnp.concatenate([hit, hit], axis=1)


def body(raw, range_filter, recon, rcmc_coef, band_offset, band_width, az_filter):
    ch = lax.axis_index("ch")
    blocks = lax.axis_size(BLK)
    raw_rows = raw.reshape(16, 4, 2, 32, 128).transpose(0, 1, 3, 2, 4).reshape(64, 64, 128)
    filt_rows = range_filter.reshape(2, 32, 128).transpose(1, 0, 2).reshape(64, 128)
    pieces = compress(raw_rows, filt_rows)
    (pieces, recon, rcmc_coef, az_filter, band_offset) = lax.optimization_barrier(
        (pieces, recon, rcmc_coef, az_filter, band_offset)
    )
    turned = lax.all_to_all(pieces, TURN, split_axis=0, concat_axis=0, tiled=True)
    weights = recon.reshape(2, 8, 128, 16).transpose(0, 1, 3, 2)
    coef = rcmc_coef.reshape(REACH, 128, 16).transpose(0, 2, 1)
    az = az_filter.reshape(2, 128, 16, 16).transpose(0, 2, 3, 1)
    select = tap_select(band_offset, band_width, ch)
    turned, weights, coef, az, select = lax.optimization_barrier(
        (turned, weights, coef, az, select)
    )
    own, near, far = doppler_mix(ch.reshape(1), turned, weights)

    total = 2 * blocks
    cross = [(i, i + 1 if i % 2 else i - 1) for i in range(total)]
    cross = [(s, d) for s, d in cross if 0 <= d < total]
    far = lax.ppermute(far, EVERY, cross)
    near = lax.ppermute(near, "ch", [(0, 1), (1, 0)])
    image = focus(own, near, far, select, coef, az)
    return image.transpose(0, 2, 1)


def solution(mesh):
    grid = jax.sharding.Mesh(mesh.devices.reshape(4, 4, 8, 2), EVERY)
    return jax.shard_map(
        body,
        mesh=grid,
        in_specs=(
            P(BLK, "ch", None, None),
            P(),
            P(),
            P(),
            P(EVERY),
            P(EVERY),
            P(None, None, EVERY),
        ),
        out_specs=P(None, None, EVERY),
        check_vma=False,
    )
```

```python
import functools
import math

import jax
import jax.numpy as jnp
import ml_dtypes
import numpy as np
from jax import lax
from jax.experimental import pallas as pl
from jax.experimental.pallas import tpu as pltpu
from jax.sharding import PartitionSpec as P

REACH = 8
BF16 = jnp.bfloat16
F32 = jnp.float32
RANGE_VMEM = 60 * 2**20
UNROLL = 16
PITCH = 264
CHIP = np.arange(128).reshape(4, 4, 8).transpose(0, 2, 1).reshape(128)
PLACE = np.argsort(CHIP)
TURN = ("ch", "x", "z", "y")
BLK = ("x", "y", "z")
EVERY = ("x", "y", "z", "ch")


def phase(rows, cols, length, sign):
    angle = sign * 2.0 * np.pi * ((np.outer(rows, cols) % length) / length)
    return np.cos(angle), np.sin(angle)


def pair(table):
    high = table.astype(np.float32).astype(ml_dtypes.bfloat16)
    low = (table - high.astype(np.float64)).astype(np.float32).astype(ml_dtypes.bfloat16)
    return high, low


def as_left(table):
    high, low = pair(table)
    return np.concatenate([high, high, low], axis=1)


def as_right(table):
    high, low = pair(table)
    return np.concatenate([high, high, low], axis=0)


def right_matrix(cosine, sine, scale=1.0):
    return np.block([[cosine, sine], [-sine, cosine]]) * scale


@functools.cache
def range_tables():
    t = np.arange(32)
    lane = np.arange(128)
    twist_in = np.stack(phase(t, lane, 4096, -1)).astype(np.float32)
    kl = 4 * (lane % 32) + lane // 32
    second = as_right(right_matrix(*phase(lane, kl, 128, -1)))
    third = as_right(right_matrix(*phase(kl, lane, 128, 1), scale=1.0 / 4096))
    twist_out = np.stack(phase(t, lane, 4096, 1)).astype(np.float32)
    matrices = np.concatenate([second, third], axis=0)
    return matrices, np.concatenate([twist_in, twist_out], axis=0)


@functools.cache
def line_tables():
    row = np.arange(128)
    fb = 16 * (row % 8) + row // 8
    c, s = phase(fb, 16 * CHIP, 2048, -1)
    high, low = pair(np.block([[c, -s], [s, c]]))
    table = np.concatenate([high, low], axis=1)
    twist = np.stack(phase(fb, np.arange(16), 2048, -1)).astype(np.float32)
    eye = np.eye(128).astype(ml_dtypes.bfloat16)
    return table, twist, np.concatenate([eye, eye], axis=1)


@functools.cache
def focus_tables():
    lane = np.arange(128)
    right = as_right(right_matrix(*phase(lane, lane, 128, 1), scale=1.0 / 2048))
    twist = np.stack(phase(np.arange(16), lane, 2048, 1)).astype(np.float32)
    return right, twist


def split(x):
    high = x.astype(BF16)
    return high, (x - high.astype(F32)).astype(BF16)


def dot(left, right):
    return jnp.dot(left, right, preferred_element_type=F32)


def left_rows(re, im):
    rh, rl = split(re)
    ih, il = split(im)
    return jnp.concatenate([rh, ih, rl, il, rh, ih], axis=1)


def right_cols(x):
    high, low = split(x)
    return jnp.concatenate([high, low, high], axis=0)


def times(ar, ai, br, bi):
    return ar * br - ai * bi, ar * bi + ai * br


def small_fft(values, sign):
    count = len(values)
    if count == 1:
        return values
    even = small_fft(values[0::2], sign)
    odd = small_fft(values[1::2], sign)
    low, high = [], []
    for k in range(count // 2):
        (er, ei), (pr, pi) = even[k], odd[k]
        if k == 0:
            tr, ti = pr, pi
        elif 4 * k == count:
            tr, ti = (-pi, pr) if sign > 0 else (pi, -pr)
        else:
            c, s = math.cos(2 * math.pi * k / count), sign * math.sin(2 * math.pi * k / count)
            tr, ti = pr * c - pi * s, pr * s + pi * c
        low.append((er + tr, ei + ti))
        high.append((er - tr, ei - ti))
    return low + high


def swap_blocks(parts):
    lane = lax.broadcasted_iota(jnp.int32, parts[0].shape, 1)
    parts = list(parts)
    for step in (4, 2, 1):
        width = 16 * step
        low = (lane // width) % 2 == 0
        for i in range(8):
            if i & step:
                continue
            p, q = parts[i], parts[i + step]
            m = jnp.where(low, q, p)
            if step == 4:
                m = pltpu.roll(m, 64, 1)
            else:
                m = jnp.take_along_axis(m, lane ^ width, axis=1)
            parts[i] = jnp.where(low, p, m)
            parts[i + step] = jnp.where(low, m, q)
    return parts


def over_rows(table, row):
    return jnp.broadcast_to(table[row : row + 1, :], (8, 128))


def range_kernel(raw, filt, matrices, twists, out, raws, mats, small, reply, kept, held, ready, gone):
    def line_copy(i):
        return raw.at[256 * i : 256 * i + 256], raws.at[PITCH * i : PITCH * i + 256]

    loads = []
    for i, (source, target) in enumerate(
        [
            *[line_copy(i) for i in range(8)],
            (twists, small),
            (filt, reply),
            (matrices, mats),
            *[line_copy(i) for i in range(8, 16)],
        ]
    ):
        copy = pltpu.make_async_copy(source, target, ready.at[i])
        copy.start()
        loads.append(copy)
    for copy in loads[:10]:
        copy.wait()
    spectrum_filter = []
    for part in range(2):
        rows = reply[pl.ds(part, 32, stride=2), :]
        tall = jnp.concatenate([rows, jnp.zeros((96, 128), F32)], axis=0).T
        total = tall[0:32]
        for m in range(1, 4):
            total = total + pltpu.roll(tall[32 * m : 32 * m + 32], 32 * m, 1)
        spectrum_filter.append(total)
    hr, hi = spectrum_filter

    def apply(values, re, im):
        return [
            times(vr, vi, over_rows(re, k), over_rows(im, k)) for k, (vr, vi) in enumerate(values)
        ]

    def lanes(values, matrix):
        y = dot(
            left_rows(
                jnp.concatenate([v[0] for v in values], axis=0),
                jnp.concatenate([v[1] for v in values], axis=0),
            ),
            matrix,
        )
        return [(y[8 * k : 8 * k + 8, :128], y[8 * k : 8 * k + 8, 128:]) for k in range(32)]

    stores = []
    for half in range(2):
        for c in range(4):
            base = half * 8 * PITCH + c * 64
            x = [
                tuple(raws[pl.ds(base + 2 * t + part, 8, stride=PITCH), :] for part in range(2))
                for t in range(32)
            ]
            x = apply(small_fft(x, -1), small[0], small[1])
            if half == 0 and c == 0:
                for copy in loads[10:]:
                    copy.wait()
            x = apply(lanes(x, mats[0:768, :]), hr, hi)
            x = apply(lanes(x, mats[768:1536, :]), small[2], small[3])
            for nt, value in enumerate(small_fft(x, 1)):
                for part in range(2):
                    kept[nt, part * 4 + c] = value[part]
        for i in range(32):
            blocks = swap_blocks([kept[i, e] for e in range(8)])
            for d, block in enumerate(blocks):
                place = int(PLACE[4 * i + d // 2]) + 128 * (d % 2)
                held[half, place] = block
            if i % 8 == 7:
                for core in range(2):
                    spot = 128 * core + 4 * (i - 7)
                    copy = pltpu.make_async_copy(
                        held.at[half, spot : spot + 32],
                        out.at[spot : spot + 32, 8 * half : 8 * half + 8, :],
                        gone.at[len(stores)],
                    )
                    copy.start()
                    stores.append(copy)
    for copy in stores:
        copy.wait()


def compress(raw_rows, filt_rows):
    matrices, twists = range_tables()
    anywhere = pl.BlockSpec(memory_space=pl.ANY)
    return pl.pallas_call(
        range_kernel,
        in_specs=[anywhere] * 4,
        out_specs=anywhere,
        out_shape=jax.ShapeDtypeStruct((256, 16, 128), F32),
        scratch_shapes=[
            pltpu.VMEM((16 * PITCH, 128), F32),
            pltpu.VMEM(matrices.shape, BF16),
            pltpu.VMEM((4, 32, 128), F32),
            pltpu.VMEM((64, 128), F32),
            pltpu.VMEM((32, 8, 8, 128), F32),
            pltpu.VMEM((2, 256, 8, 128), F32),
            pltpu.SemaphoreType.DMA((19,)),
            pltpu.SemaphoreType.DMA((16,)),
        ],
        compiler_params=pltpu.CompilerParams(vmem_limit_bytes=RANGE_VMEM),
        cost_estimate=pl.CostEstimate(flops=4 * 10**9, bytes_accessed=2**22, transcendentals=0),
        name="range_compress",
    )(raw_rows, filt_rows, matrices, twists)


def mix_kernel(ch, turned, table, twist, eye, weights, own, near, far, held):
    low = lax.broadcasted_iota(jnp.int32, (128, 128), 1) < 64
    f = table[...]
    f = jnp.concatenate([f[:, :256], f], axis=1)
    for j in range(0, 16, 2):
        cols = []
        for line in (j, j + 1):
            a, b = turned[0:128, line, :], turned[128:256, line, :]
            m = pltpu.roll(jnp.where(low, b, a), 64, 1)
            cols.append(jnp.concatenate([jnp.where(low, a, m), jnp.where(low, m, b)], axis=0))
        y = dot(f, right_cols(jnp.concatenate(cols, axis=1)))
        for k in range(2):
            re, im = y[:128, 128 * k : 128 * k + 128], y[128:, 128 * k : 128 * k + 128]
            if j + k:
                re, im = times(re, im, twist[0, :, j + k : j + k + 1], twist[1, :, j + k : j + k + 1])
            held[j + k, 0] = re
            held[j + k, 1] = im

    low_core = ch[0] == 0

    def step(q, carry):
        rows = pl.ds(pl.multiple_of(q * 8, 8), 8)
        lines = [(held[j, 0, rows, :], held[j, 1, rows, :]) for j in range(16)]
        spectrum = small_fft(lines, -1)
        re = jnp.concatenate([v[0] for v in spectrum], axis=0)
        im = jnp.concatenate([v[1] for v in spectrum], axis=0)
        high, rest = split(jnp.concatenate([re, im], axis=0))
        flat = lax.dot_general(
            eye[...],
            jnp.concatenate([high, rest], axis=1),
            (((1,), (1,)), ((), ())),
            preferred_element_type=F32,
        )
        mr = mi = None
        for c in range(8):
            dr, di = flat[16 * c : 16 * c + 16, :128], flat[16 * c : 16 * c + 16, 128:]
            wr, wi = weights[0, c, pl.ds(q, 1), :], weights[1, c, pl.ds(q, 1), :]
            pr, pi = times(dr, di, wr, wi)
            mr, mi = (pr, pi) if mr is None else (mr + pr, mi + pi)
        for part, m in enumerate((mr, mi)):
            own[q, part] = m
            near[q, part] = jnp.where(low_core, m[8:], m[:8])
            far[q, part] = jnp.where(low_core, m[:8], m[8:])
        return carry

    lax.fori_loop(0, 16, step, 0, unroll=UNROLL)


def doppler_mix(ch, turned, weights):
    table, twist, eye = line_tables()
    wide = jax.ShapeDtypeStruct((16, 2, 16, 128), F32)
    thin = jax.ShapeDtypeStruct((16, 2, 8, 128), F32)
    inside = pl.BlockSpec(memory_space=pltpu.VMEM)
    return pl.pallas_call(
        mix_kernel,
        in_specs=[pl.BlockSpec(memory_space=pltpu.SMEM)] + [inside] * 5,
        out_specs=[inside] * 3,
        out_shape=[wide, thin, thin],
        scratch_shapes=[pltpu.VMEM((16, 2, 128, 128), F32)],
        compiler_params=pltpu.CompilerParams(vmem_limit_bytes=24 * 2**20),
        cost_estimate=pl.CostEstimate(flops=4 * 10**9, bytes_accessed=2**22, transcendentals=0),
        name="doppler_mix",
    )(ch, turned, table, twist, eye, weights)


def focus_kernel(own, near, far, select, coef, az, right, twist, out, held):
    def step(q, carry):
        cols = []
        for part in range(2):
            cols.append(jnp.concatenate([own[q, part], near[q, part], far[q, part]], axis=0))
        high, low = split(jnp.concatenate(cols, axis=1))
        taps = dot(select[...], jnp.concatenate([high, low], axis=0))
        moved = None
        for k in range(REACH):
            scale = coef[k, pl.ds(q, 1), :]
            term = taps[16 * k : 16 * k + 16] * jnp.concatenate([scale, scale], axis=1)
            moved = term if moved is None else moved + term
        fr, fi = times(moved[:, :128], moved[:, 128:], az[0, q], az[1, q])
        rows = pl.ds(pl.multiple_of(q * 16, 16), 16)
        held[0, rows, :] = fr
        held[1, rows, :] = fi
        return carry

    lax.fori_loop(0, 16, step, 0, unroll=UNROLL)
    y = dot(left_rows(held[0], held[1]), right[...])
    values = []
    for q in range(16):
        rows = y[16 * q : 16 * q + 16]
        values.append(times(rows[:, :128], rows[:, 128:], twist[0, q : q + 1], twist[1, q : q + 1]))
    for n, (re, im) in enumerate(small_fft(values, 1)):
        out[0, :, 128 * n : 128 * n + 128] = re
        out[1, :, 128 * n : 128 * n + 128] = im


def focus(own, near, far, select, coef, az):
    right, twist = focus_tables()
    return pl.pallas_call(
        focus_kernel,
        out_shape=jax.ShapeDtypeStruct((2, 16, 2048), F32),
        scratch_shapes=[pltpu.VMEM((2, 256, 128), F32)],
        compiler_params=pltpu.CompilerParams(vmem_limit_bytes=48 * 2**20),
        name="focus",
    )(own, near, far, select, coef, az, right, twist)


def tap_select(band_offset, band_width, ch):
    tap = jnp.arange(REACH, dtype=jnp.int32)[:, None, None]
    eight = jnp.arange(8, dtype=jnp.int32)
    left, right = eight, eight + 24
    row = jnp.concatenate(
        [
            eight + 8,
            eight + 16,
            jnp.where(ch == 0, right, left),
            jnp.where(ch == 0, left, right),
        ]
    )
    target = jnp.arange(16, dtype=jnp.int32)[None, :, None] + REACH + band_offset[None, :, None] + tap
    hit = (row[None, None, :] == target) & (tap < band_width[None, :, None])
    hit = hit.astype(BF16).reshape(REACH * 16, 32)
    return jnp.concatenate([hit, hit], axis=1)


def body(raw, range_filter, recon, rcmc_coef, band_offset, band_width, az_filter):
    ch = lax.axis_index("ch")
    blocks = lax.axis_size(BLK)
    raw_rows = raw.reshape(16, 4, 2, 32, 128).transpose(0, 1, 3, 2, 4).reshape(4096, 128)
    filt_rows = range_filter.reshape(2, 32, 128).transpose(1, 0, 2).reshape(64, 128)
    pieces = compress(raw_rows, filt_rows)
    (pieces, recon, rcmc_coef, az_filter, band_offset) = lax.optimization_barrier(
        (pieces, recon, rcmc_coef, az_filter, band_offset)
    )
    turned = lax.all_to_all(pieces, TURN, split_axis=0, concat_axis=0, tiled=True)
    weights = recon.reshape(2, 8, 128, 16).transpose(0, 1, 3, 2)
    coef = rcmc_coef.reshape(REACH, 128, 16).transpose(0, 2, 1)
    az = az_filter.reshape(2, 128, 16, 16).transpose(0, 2, 3, 1)
    select = tap_select(band_offset, band_width, ch)
    turned, weights, coef, az, select = lax.optimization_barrier(
        (turned, weights, coef, az, select)
    )
    own, near, far = doppler_mix(ch.reshape(1), turned, weights)

    total = 2 * blocks
    cross = [(i, i + 1 if i % 2 else i - 1) for i in range(total)]
    cross = [(s, d) for s, d in cross if 0 <= d < total]
    far = lax.ppermute(far, EVERY, cross)
    near = lax.ppermute(near, "ch", [(0, 1), (1, 0)])
    image = focus(own, near, far, select, coef, az)
    return image.transpose(0, 2, 1)


def solution(mesh):
    grid = jax.sharding.Mesh(mesh.devices.reshape(4, 4, 8, 2), EVERY)
    return jax.shard_map(
        body,
        mesh=grid,
        in_specs=(
            P(BLK, "ch", None, None),
            P(),
            P(),
            P(),
            P(EVERY),
            P(EVERY),
            P(None, None, EVERY),
        ),
        out_specs=P(None, None, EVERY),
        check_vma=False,
    )
```

```python
import functools
import math

import jax
import jax.numpy as jnp
import ml_dtypes
import numpy as np
from jax import lax
from jax.experimental import pallas as pl
from jax.experimental.pallas import tpu as pltpu
from jax.sharding import PartitionSpec as P

REACH = 8
BF16 = jnp.bfloat16
F32 = jnp.float32
RANGE_VMEM = 60 * 2**20
UNROLL = 16
PITCH = 264
CHIP = np.arange(128).reshape(4, 4, 8).transpose(0, 2, 1).reshape(128)
PLACE = np.argsort(CHIP)
TURN = ("ch", "x", "z", "y")
BLK = ("x", "y", "z")
EVERY = ("x", "y", "z", "ch")


def phase(rows, cols, length, sign):
    angle = sign * 2.0 * np.pi * ((np.outer(rows, cols) % length) / length)
    return np.cos(angle), np.sin(angle)


def pair(table):
    high = table.astype(np.float32).astype(ml_dtypes.bfloat16)
    low = (table - high.astype(np.float64)).astype(np.float32).astype(ml_dtypes.bfloat16)
    return high, low


def as_left(table):
    high, low = pair(table)
    return np.concatenate([high, high, low], axis=1)


def as_right(table):
    high, low = pair(table)
    return np.concatenate([high, high, low], axis=0)


def right_matrix(cosine, sine, scale=1.0):
    return np.block([[cosine, sine], [-sine, cosine]]) * scale


@functools.cache
def range_tables():
    t = np.arange(32)
    lane = np.arange(128)
    twist_in = np.stack(phase(t, lane, 4096, -1)).astype(np.float32)
    kl = 4 * (lane % 32) + lane // 32
    second = as_right(right_matrix(*phase(lane, kl, 128, -1)))
    third = as_right(right_matrix(*phase(kl, lane, 128, 1), scale=1.0 / 4096))
    twist_out = np.stack(phase(t, lane, 4096, 1)).astype(np.float32)
    matrices = np.concatenate([second, third], axis=0)
    return matrices, np.concatenate([twist_in, twist_out], axis=0)


@functools.cache
def line_tables():
    row = np.arange(128)
    fb = 16 * (row % 8) + row // 8
    c, s = phase(fb, 16 * CHIP, 2048, -1)
    high, low = pair(np.block([[c, -s], [s, c]]))
    table = np.concatenate([high, low], axis=1)
    twist = np.stack(phase(fb, np.arange(16), 2048, -1)).astype(np.float32)
    eye = np.eye(128).astype(ml_dtypes.bfloat16)
    return table, twist, np.concatenate([eye, eye], axis=1)


@functools.cache
def focus_tables():
    lane = np.arange(128)
    right = as_right(right_matrix(*phase(lane, lane, 128, 1), scale=1.0 / 2048))
    twist = np.stack(phase(np.arange(16), lane, 2048, 1)).astype(np.float32)
    return right, twist


def split(x):
    high = x.astype(BF16)
    return high, (x - high.astype(F32)).astype(BF16)


def dot(left, right):
    return jnp.dot(left, right, preferred_element_type=F32)


def left_rows(re, im):
    rh, rl = split(re)
    ih, il = split(im)
    return jnp.concatenate([rh, ih, rl, il, rh, ih], axis=1)


def right_cols(x):
    high, low = split(x)
    return jnp.concatenate([high, low, high], axis=0)


def times(ar, ai, br, bi):
    return ar * br - ai * bi, ar * bi + ai * br


def small_fft(values, sign):
    count = len(values)
    if count == 1:
        return values
    even = small_fft(values[0::2], sign)
    odd = small_fft(values[1::2], sign)
    low, high = [], []
    for k in range(count // 2):
        (er, ei), (pr, pi) = even[k], odd[k]
        if k == 0:
            tr, ti = pr, pi
        elif 4 * k == count:
            tr, ti = (-pi, pr) if sign > 0 else (pi, -pr)
        else:
            c, s = math.cos(2 * math.pi * k / count), sign * math.sin(2 * math.pi * k / count)
            tr, ti = pr * c - pi * s, pr * s + pi * c
        low.append((er + tr, ei + ti))
        high.append((er - tr, ei - ti))
    return low + high


def swap_blocks(parts):
    lane = lax.broadcasted_iota(jnp.int32, parts[0].shape, 1)
    parts = list(parts)
    for step in (4, 2, 1):
        width = 16 * step
        low = (lane // width) % 2 == 0
        for i in range(8):
            if i & step:
                continue
            p, q = parts[i], parts[i + step]
            m = jnp.where(low, q, p)
            if step == 4:
                m = pltpu.roll(m, 64, 1)
            else:
                m = jnp.take_along_axis(m, lane ^ width, axis=1)
            parts[i] = jnp.where(low, p, m)
            parts[i + step] = jnp.where(low, m, q)
    return parts


def over_rows(table, row):
    return jnp.broadcast_to(table[row : row + 1, :], (8, 128))


def range_kernel(raw, filt, matrices, twists, out, raws, mats, small, reply, kept, held, ready, gone):
    def line_copy(i):
        return raw.at[256 * i : 256 * i + 256], raws.at[PITCH * i : PITCH * i + 256]

    loads = []
    for i, (source, target) in enumerate(
        [
            *[line_copy(i) for i in range(8)],
            (twists, small),
            (filt, reply),
            (matrices, mats),
            *[line_copy(i) for i in range(8, 16)],
        ]
    ):
        copy = pltpu.make_async_copy(source, target, ready.at[i])
        copy.start()
        loads.append(copy)
    for copy in loads[:10]:
        copy.wait()
    spectrum_filter = []
    for part in range(2):
        rows = reply[pl.ds(part, 32, stride=2), :]
        tall = jnp.concatenate([rows, jnp.zeros((96, 128), F32)], axis=0).T
        total = tall[0:32]
        for m in range(1, 4):
            total = total + pltpu.roll(tall[32 * m : 32 * m + 32], 32 * m, 1)
        spectrum_filter.append(total)
    hr, hi = spectrum_filter

    def apply(values, re, im):
        return [
            times(vr, vi, over_rows(re, k), over_rows(im, k)) for k, (vr, vi) in enumerate(values)
        ]

    def lanes(values, matrix):
        y = dot(
            left_rows(
                jnp.concatenate([v[0] for v in values], axis=0),
                jnp.concatenate([v[1] for v in values], axis=0),
            ),
            matrix,
        )
        return [(y[8 * k : 8 * k + 8, :128], y[8 * k : 8 * k + 8, 128:]) for k in range(32)]

    stores = []
    for half in range(2):
        for c in range(4):
            base = half * 8 * PITCH + c * 64
            x = [
                tuple(raws[pl.ds(base + 2 * t + part, 8, stride=PITCH), :] for part in range(2))
                for t in range(32)
            ]
            x = apply(small_fft(x, -1), small[0], small[1])
            if half == 0 and c == 0:
                for copy in loads[10:]:
                    copy.wait()
            x = apply(lanes(x, mats[0:768, :]), hr, hi)
            x = apply(lanes(x, mats[768:1536, :]), small[2], small[3])
            for nt, value in enumerate(small_fft(x, 1)):
                for part in range(2):
                    kept[nt, part * 4 + c] = value[part]
        for i in range(32):
            blocks = swap_blocks([kept[i, e] for e in range(8)])
            for d, block in enumerate(blocks):
                place = int(PLACE[4 * i + d // 2]) + 128 * (d % 2)
                held[half, place] = block
            if i % 8 == 7:
                for core in range(2):
                    spot = 128 * core + 4 * (i - 7)
                    copy = pltpu.make_async_copy(
                        held.at[half, spot : spot + 32],
                        out.at[spot : spot + 32, 8 * half : 8 * half + 8, :],
                        gone.at[len(stores)],
                    )
                    copy.start()
                    stores.append(copy)
    for copy in stores:
        copy.wait()


def compress(raw_rows, filt_rows):
    matrices, twists = range_tables()
    anywhere = pl.BlockSpec(memory_space=pl.ANY)
    return pl.pallas_call(
        range_kernel,
        in_specs=[anywhere] * 4,
        out_specs=anywhere,
        out_shape=jax.ShapeDtypeStruct((256, 16, 128), F32),
        scratch_shapes=[
            pltpu.VMEM((16 * PITCH, 128), F32),
            pltpu.VMEM(matrices.shape, BF16),
            pltpu.VMEM((4, 32, 128), F32),
            pltpu.VMEM((64, 128), F32),
            pltpu.VMEM((32, 8, 8, 128), F32),
            pltpu.VMEM((2, 256, 8, 128), F32),
            pltpu.SemaphoreType.DMA((19,)),
            pltpu.SemaphoreType.DMA((16,)),
        ],
        compiler_params=pltpu.CompilerParams(vmem_limit_bytes=RANGE_VMEM),
        cost_estimate=pl.CostEstimate(flops=4 * 10**9, bytes_accessed=2**22, transcendentals=0),
        name="range_compress",
    )(raw_rows, filt_rows, matrices, twists)


def mix_kernel(ch, turned, table, twist, eye, weights, own, near, far, held):
    low = lax.broadcasted_iota(jnp.int32, (128, 128), 1) < 64
    f = table[...]
    f = jnp.concatenate([f[:, :256], f], axis=1)
    for j in range(0, 16, 2):
        cols = []
        for line in (j, j + 1):
            a, b = turned[pl.ds(line, 128, stride=16), :], turned[pl.ds(2048 + line, 128, stride=16), :]
            m = pltpu.roll(jnp.where(low, b, a), 64, 1)
            cols.append(jnp.concatenate([jnp.where(low, a, m), jnp.where(low, m, b)], axis=0))
        y = dot(f, right_cols(jnp.concatenate(cols, axis=1)))
        for k in range(2):
            re, im = y[:128, 128 * k : 128 * k + 128], y[128:, 128 * k : 128 * k + 128]
            if j + k:
                re, im = times(re, im, twist[0, :, j + k : j + k + 1], twist[1, :, j + k : j + k + 1])
            held[j + k, 0] = re
            held[j + k, 1] = im

    low_core = ch[0] == 0

    def step(q, carry):
        rows = pl.ds(pl.multiple_of(q * 8, 8), 8)
        lines = [(held[j, 0, rows, :], held[j, 1, rows, :]) for j in range(16)]
        spectrum = small_fft(lines, -1)
        re = jnp.concatenate([v[0] for v in spectrum], axis=0)
        im = jnp.concatenate([v[1] for v in spectrum], axis=0)
        high, rest = split(jnp.concatenate([re, im], axis=0))
        flat = lax.dot_general(
            eye[...],
            jnp.concatenate([high, rest], axis=1),
            (((1,), (1,)), ((), ())),
            preferred_element_type=F32,
        )
        mr = mi = None
        for c in range(8):
            dr, di = flat[16 * c : 16 * c + 16, :128], flat[16 * c : 16 * c + 16, 128:]
            wr, wi = weights[0, c, pl.ds(q, 1), :], weights[1, c, pl.ds(q, 1), :]
            pr, pi = times(dr, di, wr, wi)
            mr, mi = (pr, pi) if mr is None else (mr + pr, mi + pi)
        for part, m in enumerate((mr, mi)):
            own[q, part] = m
            near[q, part] = jnp.where(low_core, m[8:], m[:8])
            far[q, part] = jnp.where(low_core, m[:8], m[8:])
        return carry

    lax.fori_loop(0, 16, step, 0, unroll=UNROLL)


def doppler_mix(ch, turned, weights):
    table, twist, eye = line_tables()
    wide = jax.ShapeDtypeStruct((16, 2, 16, 128), F32)
    thin = jax.ShapeDtypeStruct((16, 2, 8, 128), F32)
    inside = pl.BlockSpec(memory_space=pltpu.VMEM)
    return pl.pallas_call(
        mix_kernel,
        in_specs=[pl.BlockSpec(memory_space=pltpu.SMEM)] + [inside] * 5,
        out_specs=[inside] * 3,
        out_shape=[wide, thin, thin],
        scratch_shapes=[pltpu.VMEM((16, 2, 128, 128), F32)],
        compiler_params=pltpu.CompilerParams(vmem_limit_bytes=24 * 2**20),
        cost_estimate=pl.CostEstimate(flops=4 * 10**9, bytes_accessed=2**22, transcendentals=0),
        name="doppler_mix",
    )(ch, turned.reshape(4096, 128), table, twist, eye, weights)


def focus_kernel(own, near, far, select, coef, az, right, twist, out, held):
    def step(q, carry):
        cols = []
        for part in range(2):
            cols.append(jnp.concatenate([own[q, part], near[q, part], far[q, part]], axis=0))
        high, low = split(jnp.concatenate(cols, axis=1))
        taps = dot(select[...], jnp.concatenate([high, low], axis=0))
        moved = None
        for k in range(REACH):
            scale = coef[k, pl.ds(q, 1), :]
            term = taps[16 * k : 16 * k + 16] * jnp.concatenate([scale, scale], axis=1)
            moved = term if moved is None else moved + term
        fr, fi = times(moved[:, :128], moved[:, 128:], az[0, q], az[1, q])
        rows = pl.ds(pl.multiple_of(q * 16, 16), 16)
        held[0, rows, :] = fr
        held[1, rows, :] = fi
        return carry

    lax.fori_loop(0, 16, step, 0, unroll=UNROLL)
    y = dot(left_rows(held[0], held[1]), right[...])
    values = []
    for q in range(16):
        rows = y[16 * q : 16 * q + 16]
        values.append(times(rows[:, :128], rows[:, 128:], twist[0, q : q + 1], twist[1, q : q + 1]))
    for n, (re, im) in enumerate(small_fft(values, 1)):
        out[0, :, 128 * n : 128 * n + 128] = re
        out[1, :, 128 * n : 128 * n + 128] = im


def focus(own, near, far, select, coef, az):
    right, twist = focus_tables()
    return pl.pallas_call(
        focus_kernel,
        out_shape=jax.ShapeDtypeStruct((2, 16, 2048), F32),
        scratch_shapes=[pltpu.VMEM((2, 256, 128), F32)],
        compiler_params=pltpu.CompilerParams(vmem_limit_bytes=48 * 2**20),
        name="focus",
    )(own, near, far, select, coef, az, right, twist)


def tap_select(band_offset, band_width, ch):
    tap = jnp.arange(REACH, dtype=jnp.int32)[:, None, None]
    eight = jnp.arange(8, dtype=jnp.int32)
    left, right = eight, eight + 24
    row = jnp.concatenate(
        [
            eight + 8,
            eight + 16,
            jnp.where(ch == 0, right, left),
            jnp.where(ch == 0, left, right),
        ]
    )
    target = jnp.arange(16, dtype=jnp.int32)[None, :, None] + REACH + band_offset[None, :, None] + tap
    hit = (row[None, None, :] == target) & (tap < band_width[None, :, None])
    hit = hit.astype(BF16).reshape(REACH * 16, 32)
    return jnp.concatenate([hit, hit], axis=1)


def body(raw, range_filter, recon, rcmc_coef, band_offset, band_width, az_filter):
    ch = lax.axis_index("ch")
    blocks = lax.axis_size(BLK)
    raw_rows = raw.reshape(16, 4, 2, 32, 128).transpose(0, 1, 3, 2, 4).reshape(4096, 128)
    filt_rows = range_filter.reshape(2, 32, 128).transpose(1, 0, 2).reshape(64, 128)
    pieces = compress(raw_rows, filt_rows)
    (pieces, recon, rcmc_coef, az_filter, band_offset) = lax.optimization_barrier(
        (pieces, recon, rcmc_coef, az_filter, band_offset)
    )
    turned = lax.all_to_all(pieces, TURN, split_axis=0, concat_axis=0, tiled=True)
    weights = recon.reshape(2, 8, 128, 16).transpose(0, 1, 3, 2)
    coef = rcmc_coef.reshape(REACH, 128, 16).transpose(0, 2, 1)
    az = az_filter.reshape(2, 128, 16, 16).transpose(0, 2, 3, 1)
    select = tap_select(band_offset, band_width, ch)
    turned, weights, coef, az, select = lax.optimization_barrier(
        (turned, weights, coef, az, select)
    )
    own, near, far = doppler_mix(ch.reshape(1), turned, weights)

    total = 2 * blocks
    cross = [(i, i + 1 if i % 2 else i - 1) for i in range(total)]
    cross = [(s, d) for s, d in cross if 0 <= d < total]
    far = lax.ppermute(far, EVERY, cross)
    near = lax.ppermute(near, "ch", [(0, 1), (1, 0)])
    image = focus(own, near, far, select, coef, az)
    return image.transpose(0, 2, 1)


def solution(mesh):
    grid = jax.sharding.Mesh(mesh.devices.reshape(4, 4, 8, 2), EVERY)
    return jax.shard_map(
        body,
        mesh=grid,
        in_specs=(
            P(BLK, "ch", None, None),
            P(),
            P(),
            P(),
            P(EVERY),
            P(EVERY),
            P(None, None, EVERY),
        ),
        out_specs=P(None, None, EVERY),
        check_vma=False,
    )
```

```python
import functools
import math

import jax
import jax.numpy as jnp
import ml_dtypes
import numpy as np
from jax import lax
from jax.experimental import pallas as pl
from jax.experimental.pallas import tpu as pltpu
from jax.sharding import PartitionSpec as P

REACH = 8
BF16 = jnp.bfloat16
F32 = jnp.float32
RANGE_VMEM = 60 * 2**20
UNROLL = 16
PITCH = 264
CHIP = np.arange(128).reshape(4, 4, 8).transpose(1, 2, 0).reshape(128)
PLACE = np.argsort(CHIP)
TURN = ("ch", "y", "z", "x")
BLK = ("x", "y", "z")
EVERY = ("x", "y", "z", "ch")


def phase(rows, cols, length, sign):
    angle = sign * 2.0 * np.pi * ((np.outer(rows, cols) % length) / length)
    return np.cos(angle), np.sin(angle)


def pair(table):
    high = table.astype(np.float32).astype(ml_dtypes.bfloat16)
    low = (table - high.astype(np.float64)).astype(np.float32).astype(ml_dtypes.bfloat16)
    return high, low


def as_left(table):
    high, low = pair(table)
    return np.concatenate([high, high, low], axis=1)


def as_right(table):
    high, low = pair(table)
    return np.concatenate([high, high, low], axis=0)


def right_matrix(cosine, sine, scale=1.0):
    return np.block([[cosine, sine], [-sine, cosine]]) * scale


@functools.cache
def range_tables():
    t = np.arange(32)
    lane = np.arange(128)
    twist_in = np.stack(phase(t, lane, 4096, -1)).astype(np.float32)
    kl = 4 * (lane % 32) + lane // 32
    second = as_right(right_matrix(*phase(lane, kl, 128, -1)))
    third = as_right(right_matrix(*phase(kl, lane, 128, 1), scale=1.0 / 4096))
    twist_out = np.stack(phase(t, lane, 4096, 1)).astype(np.float32)
    matrices = np.concatenate([second, third], axis=0)
    return matrices, np.concatenate([twist_in, twist_out], axis=0)


@functools.cache
def line_tables():
    row = np.arange(128)
    fb = 16 * (row % 8) + row // 8
    c, s = phase(fb, 16 * CHIP, 2048, -1)
    high, low = pair(np.block([[c, -s], [s, c]]))
    table = np.concatenate([high, low], axis=1)
    twist = np.stack(phase(fb, np.arange(16), 2048, -1)).astype(np.float32)
    eye = np.eye(128).astype(ml_dtypes.bfloat16)
    return table, twist, np.concatenate([eye, eye], axis=1)


@functools.cache
def focus_tables():
    lane = np.arange(128)
    right = as_right(right_matrix(*phase(lane, lane, 128, 1), scale=1.0 / 2048))
    twist = np.stack(phase(np.arange(16), lane, 2048, 1)).astype(np.float32)
    return right, twist


def split(x):
    high = x.astype(BF16)
    return high, (x - high.astype(F32)).astype(BF16)


def dot(left, right):
    return jnp.dot(left, right, preferred_element_type=F32)


def left_rows(re, im):
    rh, rl = split(re)
    ih, il = split(im)
    return jnp.concatenate([rh, ih, rl, il, rh, ih], axis=1)


def right_cols(x):
    high, low = split(x)
    return jnp.concatenate([high, low, high], axis=0)


def times(ar, ai, br, bi):
    return ar * br - ai * bi, ar * bi + ai * br


def small_fft(values, sign):
    count = len(values)
    if count == 1:
        return values
    even = small_fft(values[0::2], sign)
    odd = small_fft(values[1::2], sign)
    low, high = [], []
    for k in range(count // 2):
        (er, ei), (pr, pi) = even[k], odd[k]
        if k == 0:
            tr, ti = pr, pi
        elif 4 * k == count:
            tr, ti = (-pi, pr) if sign > 0 else (pi, -pr)
        else:
            c, s = math.cos(2 * math.pi * k / count), sign * math.sin(2 * math.pi * k / count)
            tr, ti = pr * c - pi * s, pr * s + pi * c
        low.append((er + tr, ei + ti))
        high.append((er - tr, ei - ti))
    return low + high


def swap_blocks(parts):
    lane = lax.broadcasted_iota(jnp.int32, parts[0].shape, 1)
    parts = list(parts)
    for step in (4, 2, 1):
        width = 16 * step
        low = (lane // width) % 2 == 0
        for i in range(8):
            if i & step:
                continue
            p, q = parts[i], parts[i + step]
            m = jnp.where(low, q, p)
            if step == 4:
                m = pltpu.roll(m, 64, 1)
            else:
                m = jnp.take_along_axis(m, lane ^ width, axis=1)
            parts[i] = jnp.where(low, p, m)
            parts[i + step] = jnp.where(low, m, q)
    return parts


def over_rows(table, row):
    return jnp.broadcast_to(table[row : row + 1, :], (8, 128))


def range_kernel(raw, filt, matrices, twists, out, raws, mats, small, reply, kept, held, ready, gone):
    def line_copy(i):
        return raw.at[256 * i : 256 * i + 256], raws.at[PITCH * i : PITCH * i + 256]

    loads = []
    for i, (source, target) in enumerate(
        [
            *[line_copy(i) for i in range(8)],
            (twists, small),
            (filt, reply),
            (matrices, mats),
            *[line_copy(i) for i in range(8, 16)],
        ]
    ):
        copy = pltpu.make_async_copy(source, target, ready.at[i])
        copy.start()
        loads.append(copy)
    for copy in loads[:10]:
        copy.wait()
    spectrum_filter = []
    for part in range(2):
        rows = reply[pl.ds(part, 32, stride=2), :]
        tall = jnp.concatenate([rows, jnp.zeros((96, 128), F32)], axis=0).T
        total = tall[0:32]
        for m in range(1, 4):
            total = total + pltpu.roll(tall[32 * m : 32 * m + 32], 32 * m, 1)
        spectrum_filter.append(total)
    hr, hi = spectrum_filter

    def apply(values, re, im):
        return [
            times(vr, vi, over_rows(re, k), over_rows(im, k)) for k, (vr, vi) in enumerate(values)
        ]

    def lanes(values, matrix):
        y = dot(
            left_rows(
                jnp.concatenate([v[0] for v in values], axis=0),
                jnp.concatenate([v[1] for v in values], axis=0),
            ),
            matrix,
        )
        return [(y[8 * k : 8 * k + 8, :128], y[8 * k : 8 * k + 8, 128:]) for k in range(32)]

    stores = []
    for half in range(2):
        for c in range(4):
            base = half * 8 * PITCH + c * 64
            x = [
                tuple(raws[pl.ds(base + 2 * t + part, 8, stride=PITCH), :] for part in range(2))
                for t in range(32)
            ]
            x = apply(small_fft(x, -1), small[0], small[1])
            if half == 0 and c == 0:
                for copy in loads[10:]:
                    copy.wait()
            x = apply(lanes(x, mats[0:768, :]), hr, hi)
            x = apply(lanes(x, mats[768:1536, :]), small[2], small[3])
            for nt, value in enumerate(small_fft(x, 1)):
                for part in range(2):
                    kept[nt, part * 4 + c] = value[part]
        for i in range(32):
            blocks = swap_blocks([kept[i, e] for e in range(8)])
            for d, block in enumerate(blocks):
                place = int(PLACE[4 * i + d // 2]) + 128 * (d % 2)
                held[half, place] = block
        copy = pltpu.make_async_copy(
            held.at[half], out.at[:, 8 * half : 8 * half + 8, :], gone.at[half]
        )
        copy.start()
        stores.append(copy)
    for copy in stores:
        copy.wait()


def compress(raw_rows, filt_rows):
    matrices, twists = range_tables()
    anywhere = pl.BlockSpec(memory_space=pl.ANY)
    return pl.pallas_call(
        range_kernel,
        in_specs=[anywhere] * 4,
        out_specs=anywhere,
        out_shape=jax.ShapeDtypeStruct((256, 16, 128), F32),
        scratch_shapes=[
            pltpu.VMEM((16 * PITCH, 128), F32),
            pltpu.VMEM(matrices.shape, BF16),
            pltpu.VMEM((4, 32, 128), F32),
            pltpu.VMEM((64, 128), F32),
            pltpu.VMEM((32, 8, 8, 128), F32),
            pltpu.VMEM((2, 256, 8, 128), F32),
            pltpu.SemaphoreType.DMA((19,)),
            pltpu.SemaphoreType.DMA((2,)),
        ],
        compiler_params=pltpu.CompilerParams(vmem_limit_bytes=RANGE_VMEM),
        cost_estimate=pl.CostEstimate(flops=4 * 10**9, bytes_accessed=2**22, transcendentals=0),
        name="range_compress",
    )(raw_rows, filt_rows, matrices, twists)


def mix_kernel(ch, turned, table, twist, eye, weights, own, near, far, held):
    low = lax.broadcasted_iota(jnp.int32, (128, 128), 1) < 64
    f = table[...]
    f = jnp.concatenate([f[:, :256], f], axis=1)
    for j in range(0, 16, 2):
        cols = []
        for line in (j, j + 1):
            a, b = turned[pl.ds(line, 128, stride=16), :], turned[pl.ds(2048 + line, 128, stride=16), :]
            m = pltpu.roll(jnp.where(low, b, a), 64, 1)
            cols.append(jnp.concatenate([jnp.where(low, a, m), jnp.where(low, m, b)], axis=0))
        y = dot(f, right_cols(jnp.concatenate(cols, axis=1)))
        for k in range(2):
            re, im = y[:128, 128 * k : 128 * k + 128], y[128:, 128 * k : 128 * k + 128]
            if j + k:
                re, im = times(re, im, twist[0, :, j + k : j + k + 1], twist[1, :, j + k : j + k + 1])
            held[j + k, 0] = re
            held[j + k, 1] = im

    low_core = ch[0] == 0

    def step(q, carry):
        rows = pl.ds(pl.multiple_of(q * 8, 8), 8)
        lines = [(held[j, 0, rows, :], held[j, 1, rows, :]) for j in range(16)]
        spectrum = small_fft(lines, -1)
        re = jnp.concatenate([v[0] for v in spectrum], axis=0)
        im = jnp.concatenate([v[1] for v in spectrum], axis=0)
        high, rest = split(jnp.concatenate([re, im], axis=0))
        flat = lax.dot_general(
            eye[...],
            jnp.concatenate([high, rest], axis=1),
            (((1,), (1,)), ((), ())),
            preferred_element_type=F32,
        )
        mr = mi = None
        for c in range(8):
            dr, di = flat[16 * c : 16 * c + 16, :128], flat[16 * c : 16 * c + 16, 128:]
            wr, wi = weights[0, c, pl.ds(q, 1), :], weights[1, c, pl.ds(q, 1), :]
            pr, pi = times(dr, di, wr, wi)
            mr, mi = (pr, pi) if mr is None else (mr + pr, mi + pi)
        for part, m in enumerate((mr, mi)):
            own[q, part] = m
            near[q, part] = jnp.where(low_core, m[8:], m[:8])
            far[q, part] = jnp.where(low_core, m[:8], m[8:])
        return carry

    lax.fori_loop(0, 16, step, 0, unroll=UNROLL)


def doppler_mix(ch, turned, weights):
    table, twist, eye = line_tables()
    wide = jax.ShapeDtypeStruct((16, 2, 16, 128), F32)
    thin = jax.ShapeDtypeStruct((16, 2, 8, 128), F32)
    inside = pl.BlockSpec(memory_space=pltpu.VMEM)
    return pl.pallas_call(
        mix_kernel,
        in_specs=[pl.BlockSpec(memory_space=pltpu.SMEM)] + [inside] * 5,
        out_specs=[inside] * 3,
        out_shape=[wide, thin, thin],
        scratch_shapes=[pltpu.VMEM((16, 2, 128, 128), F32)],
        compiler_params=pltpu.CompilerParams(vmem_limit_bytes=24 * 2**20),
        cost_estimate=pl.CostEstimate(flops=4 * 10**9, bytes_accessed=2**22, transcendentals=0),
        name="doppler_mix",
    )(ch, turned.reshape(4096, 128), table, twist, eye, weights)


def focus_kernel(own, near, far, select, coef, az, right, twist, out, held):
    def step(q, carry):
        cols = []
        for part in range(2):
            cols.append(jnp.concatenate([own[q, part], near[q, part], far[q, part]], axis=0))
        high, low = split(jnp.concatenate(cols, axis=1))
        taps = dot(select[...], jnp.concatenate([high, low], axis=0))
        moved = None
        for k in range(REACH):
            scale = coef[k, pl.ds(q, 1), :]
            term = taps[16 * k : 16 * k + 16] * jnp.concatenate([scale, scale], axis=1)
            moved = term if moved is None else moved + term
        fr, fi = times(moved[:, :128], moved[:, 128:], az[0, q], az[1, q])
        rows = pl.ds(pl.multiple_of(q * 16, 16), 16)
        held[0, rows, :] = fr
        held[1, rows, :] = fi
        return carry

    lax.fori_loop(0, 16, step, 0, unroll=UNROLL)
    y = dot(left_rows(held[0], held[1]), right[...])
    values = []
    for q in range(16):
        rows = y[16 * q : 16 * q + 16]
        values.append(times(rows[:, :128], rows[:, 128:], twist[0, q : q + 1], twist[1, q : q + 1]))
    for n, (re, im) in enumerate(small_fft(values, 1)):
        out[0, :, 128 * n : 128 * n + 128] = re
        out[1, :, 128 * n : 128 * n + 128] = im


def focus(own, near, far, select, coef, az):
    right, twist = focus_tables()
    return pl.pallas_call(
        focus_kernel,
        out_shape=jax.ShapeDtypeStruct((2, 16, 2048), F32),
        scratch_shapes=[pltpu.VMEM((2, 256, 128), F32)],
        compiler_params=pltpu.CompilerParams(vmem_limit_bytes=48 * 2**20),
        name="focus",
    )(own, near, far, select, coef, az, right, twist)


def tap_select(band_offset, band_width, ch):
    tap = jnp.arange(REACH, dtype=jnp.int32)[:, None, None]
    eight = jnp.arange(8, dtype=jnp.int32)
    left, right = eight, eight + 24
    row = jnp.concatenate(
        [
            eight + 8,
            eight + 16,
            jnp.where(ch == 0, right, left),
            jnp.where(ch == 0, left, right),
        ]
    )
    target = jnp.arange(16, dtype=jnp.int32)[None, :, None] + REACH + band_offset[None, :, None] + tap
    hit = (row[None, None, :] == target) & (tap < band_width[None, :, None])
    hit = hit.astype(BF16).reshape(REACH * 16, 32)
    return jnp.concatenate([hit, hit], axis=1)


def body(raw, range_filter, recon, rcmc_coef, band_offset, band_width, az_filter):
    ch = lax.axis_index("ch")
    blocks = lax.axis_size(BLK)
    raw_rows = raw.reshape(16, 4, 2, 32, 128).transpose(0, 1, 3, 2, 4).reshape(4096, 128)
    filt_rows = range_filter.reshape(2, 32, 128).transpose(1, 0, 2).reshape(64, 128)
    pieces = compress(raw_rows, filt_rows)
    (pieces, recon, rcmc_coef, az_filter, band_offset) = lax.optimization_barrier(
        (pieces, recon, rcmc_coef, az_filter, band_offset)
    )
    turned = lax.all_to_all(pieces, TURN, split_axis=0, concat_axis=0, tiled=True)
    weights = recon.reshape(2, 8, 128, 16).transpose(0, 1, 3, 2)
    coef = rcmc_coef.reshape(REACH, 128, 16).transpose(0, 2, 1)
    az = az_filter.reshape(2, 128, 16, 16).transpose(0, 2, 3, 1)
    select = tap_select(band_offset, band_width, ch)
    turned, weights, coef, az, select = lax.optimization_barrier(
        (turned, weights, coef, az, select)
    )
    own, near, far = doppler_mix(ch.reshape(1), turned, weights)

    total = 2 * blocks
    cross = [(i, i + 1 if i % 2 else i - 1) for i in range(total)]
    cross = [(s, d) for s, d in cross if 0 <= d < total]
    far = lax.ppermute(far, EVERY, cross)
    near = lax.ppermute(near, "ch", [(0, 1), (1, 0)])
    image = focus(own, near, far, select, coef, az)
    return image.transpose(0, 2, 1)


def solution(mesh):
    grid = jax.sharding.Mesh(mesh.devices.reshape(4, 4, 8, 2), EVERY)
    return jax.shard_map(
        body,
        mesh=grid,
        in_specs=(
            P(BLK, "ch", None, None),
            P(),
            P(),
            P(),
            P(EVERY),
            P(EVERY),
            P(None, None, EVERY),
        ),
        out_specs=P(None, None, EVERY),
        check_vma=False,
    )
```
